256 devices in a mesh: row: 32 (over z, y), col: 8 (over x, core).
Axes of the slice: x: 4, y: 4, z: 8, core: 2. Of those that a mesh axis runs over, the one named last changes fastest.
Arguments:
- tokens: bfloat16 [512, 8192], P('row', 'col'), may hold values from -6 to 6
- gate_weight: bfloat16 [8192, 28672], P('col', 'row'), may hold values from -0.0625 to 0.0625
- up_weight: bfloat16 [8192, 28672], P('col', 'row'), may hold values from -0.0625 to 0.0625
- down_weight: bfloat16 [28672, 8192], P('row', 'col'), may hold values from -0.03125 to 0.03125
- out_grad: bfloat16 [512, 8192], P('row', 'col'), may hold values from -1.5 to 1.5
Outputs:
- mixed: bfloat16 [512, 8192], P('row', 'col')
- tokens_grad: bfloat16 [512, 8192], P('row', 'col')
- gate_grad: bfloat16 [8192, 28672], P('col', 'row')
- up_grad: bfloat16 [8192, 28672], P('col', 'row')
- down_grad: bfloat16 [28672, 8192], P('row', 'col')
The draws below stay inside these ranges and needn't reach their ends.
All inputs are finite; a program needn't handle non-finite values.
Results may differ from the reference program's by a relative error of at most 0.0049.
Values may be sent and summed in bfloat16 or wider, within the bound.
No kernel may reach another device: no remote copies, remote signals or barrier semaphores. Data moves between devices by JAX's collectives and lax.ppermute only.
A program may use at most 64 MiB of HBM per device.

```python
import jax
import jax.numpy as jnp

D = 8192
FF = 28672
TOKENS = 512


def block_levels(own_key, shape, shards, low, largest):
    factor_of = 1.0
    for position, parts in shards:
        heights = jax.random.uniform(jax.random.fold_in(jax.random.fold_in(own_key, 6), position), (parts,), jnp.float32, low / len(shards), largest / len(shards))
        factor_of = factor_of * jnp.repeat(jnp.exp(heights), shape[position] // parts).reshape((-1,) + (1,) * (len(shape) - 1 - position))
    return factor_of


def centred(key, dims, spread, reach, cuts=(), dtype=jnp.bfloat16):
    drawn = jax.random.normal(key, dims, jnp.float32) * spread
    if len(cuts) > 0:
        drawn = block_levels(key, dims, cuts, -0.22, 0.18) * drawn
    return jnp.clip(drawn, min=-reach, max=reach).astype(dtype)


def setup_inputs(seed: int = 0) -> dict:
    keys = jax.random.split(jax.random.key(seed), 6)
    return {
        "tokens": centred(keys[0], (TOKENS, D), 1.0, 6.0, ((0, 32), (1, 8))),
        "gate_weight": centred(keys[1], (D, FF), D ** -0.5, 0.0625, ((0, 8), (1, 32))),
        "up_weight": centred(keys[2], (D, FF), D ** -0.5, 0.0625, ((0, 8), (1, 32))),
        "down_weight": centred(keys[3], (FF, D), FF ** -0.5, 0.03125, ((0, 32), (1, 8))),
        "out_grad": centred(keys[4], (TOKENS, D), 0.25, 1.5, ((0, 32), (1, 8))),
    }


def reference(tokens, gate_weight, up_weight, down_weight, out_grad):
    gate_pre = jnp.dot(tokens, gate_weight, preferred_element_type=jnp.float32)
    up_pre = jnp.dot(tokens, up_weight, preferred_element_type=jnp.float32)
    sigmoid_gate = jax.nn.sigmoid(gate_pre)
    hidden = (gate_pre * sigmoid_gate * up_pre).astype(jnp.bfloat16)
    mixed = jnp.dot(hidden, down_weight, preferred_element_type=jnp.float32).astype(jnp.bfloat16)
    hidden_grad = jnp.dot(out_grad, down_weight.T, preferred_element_type=jnp.float32)
    gate_delta = (hidden_grad * up_pre * sigmoid_gate * (1.0 + gate_pre * (1.0 - sigmoid_gate))).astype(jnp.bfloat16)
    up_delta = (hidden_grad * gate_pre * sigmoid_gate).astype(jnp.bfloat16)
    down_grad = jnp.dot(hidden.T, out_grad, preferred_element_type=jnp.float32).astype(jnp.bfloat16)
    gate_grad = jnp.dot(tokens.T, gate_delta, preferred_element_type=jnp.float32).astype(jnp.bfloat16)
    up_grad = jnp.dot(tokens.T, up_delta, preferred_element_type=jnp.float32).astype(jnp.bfloat16)
    tokens_grad = (jnp.dot(gate_delta, gate_weight.T, preferred_element_type=jnp.float32)
                   + jnp.dot(up_delta, up_weight.T, preferred_element_type=jnp.float32)).astype(jnp.bfloat16)
    return mixed, tokens_grad, gate_grad, up_grad, down_grad
```

```python
import jax
import jax.numpy as jnp
from jax import lax
from jax.sharding import Mesh, PartitionSpec as P

BF = jnp.bfloat16
F32 = jnp.float32
NZ, NY, NX, NC = 8, 4, 4, 2


def dot(left, right, contract):
    return lax.dot_general(left, right, (contract, ((), ())), preferred_element_type=F32)


def z_order(c):
    return [(p + 4 * c) % NZ for p in range(NZ)]


Z_GROUPS = [[z * NC + c for z in z_order(c)] for c in range(NC)]


def z_exchange(blocks):
    return lax.all_to_all(blocks, ("z", "c"), 0, 0, axis_index_groups=Z_GROUPS, tiled=True)


def gather_z(block):
    return z_exchange(jnp.broadcast_to(block[None], (NZ,) + block.shape)).reshape(-1, block.shape[1])


def y_partner(y, x, d):
    return (y - x - d) % NY


def gather_y(block):
    return [
        lax.ppermute(block, ("y", "x"), [(y_partner(y, x, d) * NX + x, y * NX + x) for y in range(NY) for x in range(NX)])
        for d in range(NY)
    ]


def scatter_y(slots):
    parts = [
        lax.ppermute(slots[d], ("y", "x"), [(y * NX + x, y_partner(y, x, d) * NX + x) for y in range(NY) for x in range(NX)])
        for d in range(NY)
    ]
    return sum(part.astype(F32) for part in parts)


def swap_core(half):
    return lax.ppermute(half, "c", [(0, 1), (1, 0)])


def scatter_col(partial):
    rows = partial.reshape(NX, NC, 64, partial.shape[1])
    held = rows[:, 0] + swap_core(rows[:, 1].astype(BF)).astype(F32)
    total = held[0]
    for d in range(1, NX):
        total = total + lax.ppermute(held[d].astype(BF), "x", [(i, (i + d) % NX) for i in range(NX)]).astype(F32)
    return total


def gather_col(block):
    slots = [block] + [lax.ppermute(block, "x", [((i + d) % NX, i) for i in range(NX)]) for d in range(1, NX)]
    own = jnp.stack(slots)
    return jnp.stack([own, swap_core(own)], axis=1).reshape(512, block.shape[1])


def scatter_row(partial):
    slots = partial.astype(BF).reshape(NY, 128, partial.shape[1])
    held = scatter_y([slots[d] for d in range(NY)]).astype(BF)
    blocks = z_exchange(held.reshape(NZ, 16, partial.shape[1]))
    return blocks.astype(F32).sum(axis=0).astype(BF)


def body(tokens, gate_weight, up_weight, down_weight, out_grad):
    width = gate_weight.shape[1]
    panel = jnp.concatenate(gather_y(gather_z(tokens)))
    grad_panel = jnp.concatenate(gather_y(gather_z(out_grad)))
    both = scatter_col(
        jnp.concatenate(
            [dot(panel, gate_weight, ((1,), (0,))), dot(panel, up_weight, ((1,), (0,)))], axis=1
        )
    )
    gate_pre, up_pre = both[:, :width], both[:, width:]
    sigmoid_gate = jax.nn.sigmoid(gate_pre)
    hidden = (gate_pre * sigmoid_gate * up_pre).astype(BF)
    hidden_all = gather_col(hidden)
    hidden_grad = scatter_col(dot(grad_panel, down_weight, ((1,), (1,))))
    gate_delta = (
        hidden_grad * up_pre * sigmoid_gate * (1.0 + gate_pre * (1.0 - sigmoid_gate))
    ).astype(BF)
    up_delta = (hidden_grad * gate_pre * sigmoid_gate).astype(BF)
    deltas = gather_col(jnp.concatenate([gate_delta, up_delta], axis=1))
    gate_all, up_all = deltas[:, :width], deltas[:, width:]
    mixed = scatter_row(dot(hidden_all, down_weight, ((1,), (0,))))
    tokens_grad = scatter_row(
        dot(gate_all, gate_weight, ((1,), (1,))) + dot(up_all, up_weight, ((1,), (1,)))
    )
    down_grad = dot(hidden_all, grad_panel, ((0,), (0,))).astype(BF)
    gate_grad = dot(panel, gate_all, ((0,), (0,))).astype(BF)
    up_grad = dot(panel, up_all, ((0,), (0,))).astype(BF)
    return (mixed, tokens_grad, gate_grad, up_grad, down_grad)


def solution(mesh):
    fine = Mesh(mesh.devices.reshape(NZ, NY, NX, NC), ("z", "y", "x", "c"))
    rc = P(("z", "y"), ("x", "c"))
    cr = P(("x", "c"), ("z", "y"))
    return jax.shard_map(
        body,
        mesh=fine,
        in_specs=(rc, cr, cr, rc, rc),
        out_specs=(rc, rc, cr, cr, rc),
        check_vma=False,
    )
```

```python
import jax
import jax.numpy as jnp
from jax import lax
from jax.sharding import Mesh, PartitionSpec as P

BF = jnp.bfloat16
F32 = jnp.float32
NZ, NY, NX, NC = 8, 4, 4, 2


def dot(left, right, contract):
    return lax.dot_general(left, right, (contract, ((), ())), preferred_element_type=F32)


def z_exchange(blocks):
    return lax.all_to_all(blocks, "z", 0, 0, tiled=True)


def shifted(array, axis, n, d):
    return lax.ppermute(array, axis, [(i, (i + d) % n) for i in range(n)])


def turned(slots, shift):
    n = len(slots)
    turns = [jnp.stack([slots[(p + k) % n] for p in range(n)]) for k in range(n)]
    return lax.select_n(shift % n, *turns)


def behind(value, first):
    return jnp.where(jnp.abs(first) < jnp.inf, value, jnp.zeros_like(value))


def gather_y(block):
    return [block] + [shifted(block, "y", NY, -d) for d in range(1, NY)]


def gather_y_at_once(block):
    slots = lax.all_to_all(jnp.broadcast_to(block[None], (NY,) + block.shape), "y", 0, 0, tiled=True)
    return list(turned(list(slots), lax.axis_index("y")))


def halves(slots):
    low, high = jnp.concatenate(slots[:2]), jnp.concatenate(slots[2:])
    core = lax.axis_index("c")
    return lax.select_n(core, low, high), lax.select_n(core, high, low)


def swap_core(half):
    return lax.ppermute(half, "c", [(0, 1), (1, 0)])


def sum_core(own, other, weight, contract):
    received = swap_core(dot(other, weight, contract))
    return (dot(own, weight, contract) + received).reshape(NX, 64, -1)


def sum_x(*helds):
    def pick(held, d):
        return lax.dynamic_index_in_dim(held, (lax.axis_index("x") + d) % NX, axis=0, keepdims=False)

    width = helds[0].shape[2]
    parts = [
        shifted(jnp.concatenate([pick(held, d).astype(BF) for held in helds], axis=1), "x", NX, d)
        for d in range(1, NX)
    ]
    return [
        pick(held, 0) + sum(part[:, i * width : (i + 1) * width].astype(F32) for part in parts)
        for i, held in enumerate(helds)
    ]


def gather_x(block):
    return [block] + [shifted(block, "x", NX, -d) for d in range(1, NX)]


def gather_core(own):
    return jnp.concatenate(own + [swap_core(slot) for slot in own])


def ordered(own, other):
    x = lax.axis_index("x")
    return jnp.concatenate(
        [turned(list(half.reshape(NX, 64, -1)), x).reshape(256, -1) for half in (own, other)]
    )


def sum_y(partial):
    width = partial.shape[1]
    rows = partial.reshape(NC * NX, 64, width)
    x, core = lax.axis_index("x"), lax.axis_index("c")

    def slot(k):
        half = (core + k // 2) % NC
        pieces = [
            lax.dynamic_index_in_dim(rows, half * NX + (2 * (k % 2) + i + NX - x) % NX, axis=0, keepdims=False)
            for i in range(2)
        ]
        return jnp.concatenate(pieces)

    held = slot(0)
    for k in range(1, NY):
        held = held + shifted(slot(k).astype(BF), "y", NY, k).astype(F32)
    return held.astype(BF)


def body(tokens, gate_weight, up_weight, down_weight, out_grad):
    width = gate_weight.shape[1]
    pair = jnp.broadcast_to(jnp.stack([tokens, out_grad])[None], (NZ, 2) + tokens.shape)
    pair = z_exchange(pair)
    own, other = halves(gather_y(pair[:, 0].reshape(128, -1)))
    gate_held = sum_core(own, other, gate_weight, ((1,), (0,)))
    up_held = sum_core(own, other, up_weight, ((1,), (0,)))
    gate_pre, up_pre = sum_x(gate_held, up_held)
    grad_slots = gather_y_at_once(pair[:, 1].reshape(128, -1))
    grad_slots, up_held = lax.optimization_barrier((grad_slots, up_held))
    own_grad, other_grad = halves(grad_slots)
    grad_held = sum_core(
        own_grad, behind(other_grad, up_held.reshape(256, -1)[:, :1]), down_weight, ((1,), (1,))
    )
    (hidden_grad,) = sum_x(grad_held)
    sigmoid_gate = jax.nn.sigmoid(gate_pre)
    hidden = behind(gate_pre * sigmoid_gate * up_pre, grad_held[0]).astype(BF)
    hidden_slots = gather_x(hidden)
    gate_pre, up_pre, hidden_grad = lax.optimization_barrier((gate_pre, up_pre, hidden_grad))
    sigmoid_gate = jax.nn.sigmoid(gate_pre)
    gate_delta = (
        hidden_grad * up_pre * sigmoid_gate * (1.0 + gate_pre * (1.0 - sigmoid_gate))
    ).astype(BF)
    up_delta = (hidden_grad * gate_pre * sigmoid_gate).astype(BF)
    delta_slots = gather_x(jnp.concatenate([gate_delta, up_delta], axis=1))
    hidden_all = gather_core(hidden_slots)
    mixed_part = dot(hidden_all, down_weight, ((1,), (0,)))
    mixed_held = sum_y(mixed_part)
    deltas = gather_core(delta_slots)
    gate_all, up_all = deltas[:, :width], deltas[:, width:]
    tokens_held = sum_y(
        dot(gate_all, gate_weight, ((1,), (1,))) + dot(up_all, up_weight, ((1,), (1,)))
    )
    both = jnp.stack([held.reshape(NZ, 16, -1) for held in (mixed_held, tokens_held)], axis=1)
    mixed, tokens_grad = z_exchange(both).astype(F32).sum(axis=0).astype(BF)
    panel, grad_panel = ordered(own, other), ordered(own_grad, other_grad)
    down_grad = dot(hidden_all, grad_panel, ((0,), (0,))).astype(BF)
    gate_grad = dot(panel, gate_all, ((0,), (0,))).astype(BF)
    up_grad = dot(panel, up_all, ((0,), (0,))).astype(BF)
    return (mixed, tokens_grad, gate_grad, up_grad, down_grad)


def solution(mesh):
    fine = Mesh(mesh.devices.reshape(NZ, NY, NX, NC), ("z", "y", "x", "c"))
    rc = P(("z", "y"), ("x", "c"))
    cr = P(("x", "c"), ("z", "y"))
    return jax.shard_map(
        body,
        mesh=fine,
        in_specs=(rc, cr, cr, rc, rc),
        out_specs=(rc, rc, cr, cr, rc),
        check_vma=False,
    )
```

```python
import jax
import jax.numpy as jnp
from jax import lax
from jax.sharding import Mesh, PartitionSpec as P

BF = jnp.bfloat16
F32 = jnp.float32
NZ, NY, NX, NC = 8, 4, 4, 2


def dot(left, right, contract):
    return lax.dot_general(left, right, (contract, ((), ())), preferred_element_type=F32)


Z_GROUPS = [[(z + 4 * (x % 2)) % NZ * NX + x for z in range(NZ)] for x in range(NX)]


def copies_z(blocks):
    return lax.all_to_all(jnp.broadcast_to(blocks[None], (NZ,) + blocks.shape), "z", 0, 0, tiled=True)


def sum_z(blocks):
    blocks = lax.all_to_all(blocks, ("z", "x"), 0, 0, axis_index_groups=Z_GROUPS, tiled=True)
    return blocks.astype(F32).sum(axis=0).astype(BF)


def shifted(array, axis, n, d):
    return lax.ppermute(array, axis, [(i, (i + d) % n) for i in range(n)])


def crossed(array, d):
    return lax.ppermute(array, "x", [(i, i ^ d) for i in range(NX)])


def gather_y(block):
    return jnp.concatenate([block] + [shifted(block, "y", NY, -d) for d in range(1, NY)])


def halves(panel):
    core = lax.axis_index("c")
    return tuple(
        lax.dynamic_slice_in_dim(panel, start * 256, 256, axis=0) for start in (core, 1 - core)
    )


def swap_core(half):
    return lax.ppermute(half, "c", [(0, 1), (1, 0)])


def sum_core(own, other, weight, contract):
    received = swap_core(dot(other, weight, contract))
    kept = lax.optimization_barrier(dot(own, weight, contract))
    return kept.reshape(NX, 64, -1), received.reshape(NX, 64, -1)


def sum_x(*helds):
    def pick(held, d):
        kept, received = [
            lax.dynamic_index_in_dim(part, lax.axis_index("x") ^ d, axis=0, keepdims=False)
            for part in held
        ]
        return kept + received

    width = helds[0][0].shape[2]
    parts = [
        crossed(jnp.concatenate([pick(held, d).astype(BF) for held in helds], axis=1), d)
        for d in range(1, NX)
    ]
    return [
        pick(held, 0) + sum(part[:, i * width : (i + 1) * width].astype(F32) for part in parts)
        for i, held in enumerate(helds)
    ]


def behind(value, first):
    return jnp.where(jnp.abs(first) < jnp.inf, value, jnp.zeros_like(value))


def gather_x(block):
    return [block] + [crossed(block, d) for d in range(1, NX)]


def gather_core(own):
    return jnp.concatenate(own + [swap_core(slot) for slot in own])


def ordered(panel):
    out = []
    for half in halves(panel):
        chunks = half.reshape(NX, 64, -1)
        turns = [jnp.stack([chunks[d ^ k] for d in range(NX)]) for k in range(NX)]
        out.append(lax.select_n(lax.axis_index("x"), *turns).reshape(256, -1))
    return jnp.concatenate(out)


def sum_y(partial):
    x, core = lax.axis_index("x"), lax.axis_index("c")

    def slot(k):
        start = 2 * ((core + k // 2) % NC) + (k % 2 ^ x // 2)
        return lax.dynamic_slice_in_dim(partial, start * 128, 128, axis=0)

    held = slot(0)
    for k in range(1, NY):
        held = held + shifted(slot(k).astype(BF), "y", NY, k).astype(F32)
    return held.astype(BF)


def body(tokens, gate_weight, up_weight, down_weight, out_grad):
    width = gate_weight.shape[1]
    pair = copies_z(jnp.stack([tokens, out_grad]))
    panel = gather_y(pair[:, 0].reshape(128, -1))
    own, other = halves(panel)
    gate_held = sum_core(own, other, gate_weight, ((1,), (0,)))
    up_held = sum_core(own, other, up_weight, ((1,), (0,)))
    grad_panel = gather_y(pair[:, 1].reshape(128, -1))
    grad_panel, up_held = lax.optimization_barrier((grad_panel, up_held))
    own_grad, other_grad = halves(grad_panel)
    grad_held = sum_core(own_grad, other_grad, down_weight, ((1,), (1,)))
    gate_pre, up_pre = sum_x(gate_held, up_held)
    (hidden_grad,) = sum_x(grad_held)
    sigmoid_gate = jax.nn.sigmoid(gate_pre)
    hidden = behind(gate_pre * sigmoid_gate * up_pre, grad_held[1][0]).astype(BF)
    gate_pre, up_pre, hidden_grad = lax.optimization_barrier((gate_pre, up_pre, hidden_grad))
    sigmoid_gate = jax.nn.sigmoid(gate_pre)
    gate_delta = (hidden_grad * up_pre * sigmoid_gate * (1.0 + gate_pre * (1.0 - sigmoid_gate))).astype(BF)
    up_delta = (hidden_grad * gate_pre * sigmoid_gate).astype(BF)
    hidden_slots = gather_x(hidden)
    delta_slots = gather_x(jnp.concatenate([gate_delta, up_delta], axis=1))
    hidden_all = gather_core(hidden_slots)
    mixed_held = sum_y(dot(hidden_all, down_weight, ((1,), (0,))))
    deltas = gather_core(delta_slots)
    gate_all, up_all = deltas[:, :width], deltas[:, width:]
    tokens_held = sum_y(
        dot(gate_all, gate_weight, ((1,), (1,))) + dot(up_all, up_weight, ((1,), (1,)))
    )
    both = jnp.stack([held.reshape(NZ, 16, -1) for held in (mixed_held, tokens_held)], axis=1)
    mixed, tokens_grad = sum_z(both)
    panel, grad_panel = ordered(panel), ordered(grad_panel)
    down_grad = dot(hidden_all, grad_panel, ((0,), (0,))).astype(BF)
    gate_grad = dot(panel, gate_all, ((0,), (0,))).astype(BF)
    up_grad = dot(panel, up_all, ((0,), (0,))).astype(BF)
    return (mixed, tokens_grad, gate_grad, up_grad, down_grad)


def solution(mesh):
    fine = Mesh(mesh.devices.reshape(NZ, NY, NX, NC), ("z", "y", "x", "c"))
    rc = P(("z", "y"), ("x", "c"))
    cr = P(("x", "c"), ("z", "y"))
    return jax.shard_map(
        body, mesh=fine, in_specs=(rc, cr, cr, rc, rc), out_specs=(rc, rc, cr, cr, rc), check_vma=False
    )
```

```python
import jax
import jax.numpy as jnp
from jax import lax
from jax.sharding import Mesh, PartitionSpec as P

BF = jnp.bfloat16
F32 = jnp.float32
NZ, NY, NX, NC = 8, 4, 4, 2


def dot(left, right, contract):
    return lax.dot_general(left, right, (contract, ((), ())), preferred_element_type=F32)


Z_GROUPS = [[(z + 4 * (x % 2)) % NZ * NX + x for z in range(NZ)] for x in range(NX)]


def copies_z(blocks):
    return lax.all_to_all(jnp.broadcast_to(blocks[None], (NZ,) + blocks.shape), "z", 0, 0, tiled=True)


def sum_z(blocks):
    blocks = lax.all_to_all(blocks, ("z", "x"), 0, 0, axis_index_groups=Z_GROUPS, tiled=True)
    return blocks.astype(F32).sum(axis=0).astype(BF)


def shifted(array, axis, n, d):
    return lax.ppermute(array, axis, [(i, (i + d) % n) for i in range(n)])


def crossed(array, d):
    return lax.ppermute(array, "x", [(i, i ^ d) for i in range(NX)])


def gather_y(block):
    return jnp.concatenate([block] + [shifted(block, "y", NY, -d) for d in range(1, NY)])


def halves(panel):
    core = lax.axis_index("c")
    return tuple(
        lax.dynamic_slice_in_dim(panel, start * 256, 256, axis=0) for start in (core, 1 - core)
    )


def swap_core(half):
    return lax.ppermute(half, "c", [(0, 1), (1, 0)])


def sum_core(own, other, weight, contract):
    received = swap_core(dot(other, weight, contract))
    kept = lax.optimization_barrier(dot(own, weight, contract))
    return kept.reshape(NX, 64, -1), received.reshape(NX, 64, -1)


def sum_x(*helds):
    def pick(held, d):
        kept, received = [
            lax.dynamic_index_in_dim(part, lax.axis_index("x") ^ d, axis=0, keepdims=False)
            for part in held
        ]
        return kept + received

    width = helds[0][0].shape[2]
    parts = [
        crossed(jnp.concatenate([pick(held, d).astype(BF) for held in helds], axis=1), d)
        for d in range(1, NX)
    ]
    return [
        pick(held, 0) + sum(part[:, i * width : (i + 1) * width].astype(F32) for part in parts)
        for i, held in enumerate(helds)
    ]


def behind(value, first):
    return jnp.where(jnp.abs(first) < jnp.inf, value, jnp.zeros_like(value))


def gather_x(block):
    return [block] + [crossed(block, d) for d in range(1, NX)]


def gather_core(own):
    return jnp.concatenate(own + [swap_core(slot) for slot in own])


def ordered(panel):
    out = []
    for half in halves(panel):
        chunks = half.reshape(NX, 64, -1)
        turns = [jnp.stack([chunks[d ^ k] for d in range(NX)]) for k in range(NX)]
        out.append(lax.select_n(lax.axis_index("x"), *turns).reshape(256, -1))
    return jnp.concatenate(out)


def sum_y(partial):
    x, core = lax.axis_index("x"), lax.axis_index("c")

    def slot(k):
        start = 2 * ((core + k // 2) % NC) + (k % 2 ^ x // 2)
        return lax.dynamic_slice_in_dim(partial, start * 128, 128, axis=0)

    held = slot(0)
    for k in range(1, NY):
        held = held + shifted(slot(k).astype(BF), "y", NY, k).astype(F32)
    return held.astype(BF)


def body(tokens, gate_weight, up_weight, down_weight, out_grad):
    width = gate_weight.shape[1]
    pair = copies_z(jnp.stack([tokens, out_grad]))
    panel = gather_y(pair[:, 0].reshape(128, -1))
    own, other = halves(panel)
    gate_held = sum_core(own, other, gate_weight, ((1,), (0,)))
    up_held = sum_core(own, other, up_weight, ((1,), (0,)))
    grad_panel = gather_y(pair[:, 1].reshape(128, -1))
    grad_panel, up_held = lax.optimization_barrier((grad_panel, up_held))
    own_grad, other_grad = halves(grad_panel)
    grad_held = sum_core(own_grad, other_grad, down_weight, ((1,), (1,)))
    gate_pre, up_pre = sum_x(gate_held, up_held)
    (hidden_grad,) = sum_x(grad_held)
    sigmoid_gate = jax.nn.sigmoid(gate_pre)
    hidden = behind(gate_pre * sigmoid_gate * up_pre, grad_held[1][0]).astype(BF)
    gate_pre, up_pre, hidden_grad = lax.optimization_barrier((gate_pre, up_pre, hidden_grad))
    sigmoid_gate = jax.nn.sigmoid(gate_pre)
    gate_delta = (hidden_grad * up_pre * sigmoid_gate * (1.0 + gate_pre * (1.0 - sigmoid_gate))).astype(BF)
    up_delta = (hidden_grad * gate_pre * sigmoid_gate).astype(BF)
    hidden_slots = gather_x(hidden)
    delta_slots = gather_x(jnp.concatenate([gate_delta, up_delta], axis=1))
    hidden_all = gather_core(hidden_slots)
    mixed_held = sum_y(dot(hidden_all, down_weight, ((1,), (0,))))
    deltas = gather_core(delta_slots)
    gate_all, up_all = deltas[:, :width], deltas[:, width:]
    tokens_held = sum_y(
        dot(gate_all, gate_weight, ((1,), (1,))) + dot(up_all, up_weight, ((1,), (1,)))
    )
    both = sum_z(jnp.concatenate([mixed_held, tokens_held], axis=1).reshape(NZ, 16, -1))
    mixed, tokens_grad = both[:, : both.shape[1] // 2], both[:, both.shape[1] // 2 :]
    panel, grad_panel = ordered(panel), ordered(grad_panel)
    down_grad = dot(hidden_all, grad_panel, ((0,), (0,))).astype(BF)
    gate_grad = dot(panel, gate_all, ((0,), (0,))).astype(BF)
    up_grad = dot(panel, up_all, ((0,), (0,))).astype(BF)
    return (mixed, tokens_grad, gate_grad, up_grad, down_grad)


def solution(mesh):
    fine = Mesh(mesh.devices.reshape(NZ, NY, NX, NC), ("z", "y", "x", "c"))
    rc = P(("z", "y"), ("x", "c"))
    cr = P(("x", "c"), ("z", "y"))
    return jax.shard_map(
        body, mesh=fine, in_specs=(rc, cr, cr, rc, rc), out_specs=(rc, rc, cr, cr, rc), check_vma=False
    )
```
